128 devices in a mesh: wide: 16 (over z_lo, y, core), narrow: 8 (over x, z_hi).
Axes of the slice: x: 4, y: 4, z: 4 (z_hi: 2, z_lo: 2; z = z_hi * 2 + z_lo), core: 2. Of those that a mesh axis runs over, the one named last changes fastest.
Arguments:
- embeddings: bfloat16 [512, 768], P(('wide', 'narrow')), may hold values from -6 to 6
- positives: int32 [512, 16], P(('wide', 'narrow')), may hold values from -1 to 1048575, as said below
- label_weight: bfloat16 [1048576, 768], P(('wide', 'narrow')), may hold values from -0.21875 to 0.21875
- label_bias: float32 [1048576], P(('wide', 'narrow')), may hold values from -8 to -4
Outputs:
- input_grad: float32 [512, 768], P(('wide', 'narrow'))
- weight_grad: bfloat16 [1048576, 768], P(('wide', 'narrow'))
- bias_grad: float32 [1048576], P(('wide', 'narrow'))
The draws below stay inside these ranges and needn't reach their ends.
Inputs may be any that keep to these rules, and one draw needn't show every extreme that they name: `positives`: each row holds 1 to 16 label ids in its first slots and -1 in the rest; ids may repeat within a row; the first row is full.
All inputs are finite; a program needn't handle non-finite values.
Results may differ from the reference program's by a relative error of at most 0.008.
Values may be sent and summed in bfloat16 or wider, within the bound.
A program may use at most 128 MiB of HBM per device.

```python
import jax
import jax.numpy as jnp
from jax import lax

D = 768
LBL_DEV = 8192
POS = 16
DOCS = 512
LABELS = 1048576


def draw_positives(key, part):
    key = jax.random.fold_in(key, 11)
    key_count, key_label = jax.random.split(key)
    counts = jax.random.randint(key_count, (DOCS,), 1, POS + 1)
    counts = counts.at[0].set(POS)
    counts = counts.at[DOCS - 1].set(1)
    label_ids = jax.random.randint(key_label, (DOCS, POS), 0, LABELS)
    label_ids = label_ids.at[DOCS - 1, 0].set(LABELS - 1)
    places = jnp.arange(POS, dtype=jnp.int32)[None, :]
    return jnp.where(places < counts[:, None], label_ids, -1).astype(jnp.int32)


def block_scale(key, extent, pieces, least, high):
    def one(dim, shards_of):
        draws = jax.random.uniform(jax.random.fold_in(jax.random.fold_in(key, 6), dim), (shards_of,), jnp.float32, least / len(pieces), high / len(pieces))
        return jnp.repeat(jnp.exp(draws), extent[dim] // shards_of).reshape((-1,) + (1,) * (len(extent) - dim - 1))

    factor_of = one(*pieces[0])
    for cut in pieces[1:]:
        factor_of = factor_of * one(*cut)
    return factor_of


def scatter_about(own_key, shape, spread, most, shards=(), kind=jnp.bfloat16):
    factor_of = block_scale(own_key, shape, shards, -0.22, 0.18) if shards else 1.0
    array = jax.random.normal(own_key, shape, jnp.float32) * spread * factor_of
    return jnp.minimum(jnp.maximum(array, -most), most).astype(kind)


def setup_inputs(seed: int = 0) -> dict:
    arg_keys = jax.random.split(jax.random.key(seed), 5)
    return {
        "embeddings": scatter_about(arg_keys[0], (DOCS, D), 1.0, 6.0, ((0, 128),)),
        "positives": draw_positives(jax.random.fold_in(arg_keys[4], 71), 0),
        "label_weight": scatter_about(arg_keys[2], (LABELS, D), D ** -0.5, 0.21875, ((0, 128),)),
        "label_bias": jnp.clip(-8.0 + 4.0 * jax.random.uniform(arg_keys[3], (LABELS,), jnp.float32) ** block_scale(arg_keys[3], (LABELS,), ((0, 128),), -0.2, 0.2), -8.0, -4.0),
    }


def reference(embeddings, positives, label_weight, label_bias):
    shard_count = LABELS // LBL_DEV
    blocks = label_weight.reshape(shard_count, LBL_DEV, D)
    biases = label_bias.reshape(shard_count, LBL_DEV)
    starts = (jnp.arange(shard_count, dtype=jnp.int32) * LBL_DEV).astype(jnp.int32)

    def advance(carry, inputs):
        weight, bias, start = inputs
        logits = lax.dot_general(embeddings, weight, (((1,), (1,)), ((), ())), preferred_element_type=jnp.float32) + bias[None, :]
        label_index = start + jnp.arange(LBL_DEV, dtype=jnp.int32)
        target = jnp.zeros(logits.shape, jnp.float32)
        for column in range(POS):
            target = jnp.maximum(target, (positives[:, column:column + 1] == label_index[None, :]).astype(jnp.float32))
        grad_full = jax.nn.sigmoid(logits) - target
        grad = grad_full.astype(jnp.bfloat16)
        carry = carry + jnp.dot(grad, weight, preferred_element_type=jnp.float32)
        weight_block = lax.dot_general(grad, embeddings, (((0,), (0,)), ((), ())), preferred_element_type=jnp.float32).astype(jnp.bfloat16)
        return carry, (weight_block, jnp.sum(grad_full, axis=0))

    input_grad, (weight_grads, bias_grads) = lax.scan(advance, jnp.zeros((DOCS, D), jnp.float32), (blocks, biases, starts))
    return input_grad, weight_grads.reshape(LABELS, D), bias_grads.reshape(LABELS)
```

```python
import functools

import jax
import jax.numpy as jnp
from jax import lax
from jax.experimental import pallas as pl
from jax.experimental.pallas import tpu as pltpu
from jax.sharding import PartitionSpec as P

LOG2E = 1.4426950408889634
LANES = 128
ROWS = 32
MESH = pl.DeviceIdType.MESH
BF16 = jnp.bfloat16
F32 = jnp.float32


def aligned(index, size):
    return pl.ds(pl.multiple_of(index, size), size)


def dot_nt(a, b):
    return lax.dot_general(a, b, (((1,), (1,)), ((), ())), preferred_element_type=F32)


def dot_tn(a, b):
    return lax.dot_general(a, b, (((0,), (0,)), ((), ())), preferred_element_type=F32)


def exchange_kernel(
    cfg,
    embed_ref,
    ids_ref,
    weight_hbm,
    bias_ref,
    input_grad_ref,
    bias_grad_ref,
    grad_hbm,
    embed_out,
    part_hbm,
    weight_v,
    grad_v,
    embed_v,
    bias_v,
    sums_v,
    mask_v,
    ids_near,
    ids_far,
    message32,
    message,
    gathered,
    wide32,
    logits_a,
    logits_b,
    grad_a,
    grad_b,
    acc_far,
    acc_own,
    acc_relay,
    outgoing,
    arrived,
    part_v,
    load_sem,
    store_sem,
    gather_sem,
    relay_sem,
    scatter_sem,
):
    labels, depth, tile, part_tile, part_rows, peers, narrow = cfg
    docs = embed_ref.shape[0]
    slots = ids_ref.shape[1]
    half = docs * peers
    lane_tiles = depth // LANES
    wide_index, narrow_index = lax.axis_index("wide"), lax.axis_index("narrow")
    core = lax.rem(wide_index, 2)
    chip = lax.div(wide_index, 2) * narrow + narrow_index
    label_offset = (wide_index * narrow + narrow_index) * labels
    sibling = (wide_index + 1 - 2 * core, narrow_index)

    def device_of(peer, on_core):
        return (2 * lax.div(peer, narrow) + on_core, lax.rem(peer, narrow))

    barrier = pltpu.get_barrier_semaphore()

    @pl.loop(0, peers)
    def _(i):
        pl.semaphore_signal(
            barrier,
            inc=1,
            device_id=device_of(lax.rem(chip + i, peers), 1 - core),
            device_id_type=MESH,
        )

    load = pltpu.make_async_copy(weight_hbm, weight_v, load_sem)
    load.start()

    embed = embed_ref[...].astype(F32)
    for k in range(lane_tiles):
        message32[k * docs : (k + 1) * docs, :] = embed[:, k * LANES : (k + 1) * LANES]
    ids = ids_ref[...]
    zeros = jnp.zeros((docs, LANES - 2 * slots), F32)
    high = jnp.right_shift(ids, 13).astype(F32)
    middle = (jnp.right_shift(ids, 8) & 31).astype(F32)
    low = (ids & 255).astype(F32)
    base = lane_tiles * docs
    message32[base : base + docs, :] = jnp.concatenate([high, middle, zeros], axis=1)
    message32[base + docs : base + 2 * docs, :] = jnp.concatenate([low, low, zeros], axis=1)
    message[...] = message32[...].astype(BF16)

    pl.semaphore_wait(barrier, peers)

    @pl.loop(0, peers)
    def _(i):
        pltpu.make_async_remote_copy(
            src_ref=message,
            dst_ref=gathered.at[aligned(chip * ROWS, ROWS)],
            send_sem=gather_sem.at[0],
            recv_sem=gather_sem.at[1],
            device_id=device_of(lax.rem(chip + i, peers), 1 - core),
            device_id_type=MESH,
        ).start()

    @pl.loop(0, labels // (8 * LANES))
    def _(i):
        rows = bias_ref[aligned(i * 8, 8), :] * (-LOG2E)
        for j in range(8):
            spread = jnp.broadcast_to(rows[j : j + 1, :], (LANES, LANES)).T
            bias_v[aligned(i * (8 * LANES) + j * LANES, LANES), :] = spread

    pltpu.make_async_copy(gathered, gathered, gather_sem.at[1]).wait()

    for i in range(8):
        step = peers * ROWS // 8
        wide32[i * step : (i + 1) * step, :] = gathered[i * step : (i + 1) * step, :].astype(F32)

    def picked(row):
        return wide32[pl.ds(row, peers, stride=ROWS), :]

    for k in range(lane_tiles):
        for r in range(docs):
            embed_v[r * peers : (r + 1) * peers, k * LANES : (k + 1) * LANES] = picked(
                k * docs + r
            ).astype(BF16)
    for pair in range(docs // 2):
        first = base + 2 * pair
        upper = jnp.concatenate([picked(first), picked(first + 1)], axis=0).T
        lower = jnp.concatenate([picked(first + docs), picked(first + docs + 1)], axis=0).T
        whole = upper[:slots] * 8192.0 + upper[slots : 2 * slots] * 256.0 + lower[:slots]
        ids_near[:, pair * LANES : (pair + 1) * LANES] = whole.astype(jnp.int32)

    relays = [
        pltpu.make_async_remote_copy(
            src_ref=source,
            dst_ref=target,
            send_sem=relay_sem.at[2 * n],
            recv_sem=relay_sem.at[2 * n + 1],
            device_id=sibling,
            device_id_type=MESH,
        )
        for n, (source, target) in enumerate(
            [
                (embed_v.at[0:half], embed_v.at[half : 2 * half]),
                (ids_near, ids_far),
                (acc_far, acc_relay),
            ]
        )
    ]
    relays[0].start()
    relays[1].start()

    groups = labels // 32

    def fill_mask(ids_v, chunk):
        local = ids_v[...] - label_offset
        local = jnp.where((local >= 0) & (local < labels), local, -1)
        group = jnp.right_shift(local, 5)
        bit = jnp.left_shift(jnp.ones_like(local), local & 31)

        @pl.loop(0, groups // 32)
        def _(i):
            index = lax.broadcasted_iota(jnp.int32, (32, half), 0) + i * 32
            words = jnp.zeros((32, half), jnp.int32)
            for j in range(slots):
                words = words | jnp.where(group[j : j + 1, :] == index, bit[j : j + 1, :], 0)
            mask_v[aligned(i * 32, 32), :] = words

    def run_chunk(chunk, acc):
        acc[...] = jnp.zeros_like(acc)
        columns = slice(chunk * half, (chunk + 1) * half)

        def logits(i, out):
            out[...] = dot_nt(weight_v[aligned(i * tile, tile), :], embed_v[columns, :])

        def gradient(i, logit, out):
            bits = jnp.left_shift(1, lax.broadcasted_iota(jnp.int32, (32, LANES), 0))
            words = mask_v[aligned(i * (tile // 32), tile // 32), :]
            for g in range(tile // 32):
                rows = aligned(i * tile + g * 32, 32)
                bias = bias_v[rows, :]
                total = None
                for h in range(half // LANES):
                    lanes = slice(h * LANES, (h + 1) * LANES)
                    x = logit[g * 32 : (g + 1) * 32, lanes]
                    sigmoid = pltpu.reciprocal(
                        1.0 + jnp.exp2(x * (-LOG2E) + bias), approx=True
                    )
                    hit = (words[g : g + 1, lanes] & bits) != 0
                    full = sigmoid - jnp.where(hit, 1.0, 0.0)
                    total = full if total is None else total + full
                    rounded = full.astype(BF16)
                    out[g * 32 : (g + 1) * 32, lanes] = rounded
                    grad_v[rows, chunk * half + h * LANES : chunk * half + (h + 1) * LANES] = (
                        rounded
                    )
                if chunk == 0:
                    sums_v[rows, :] = total
                else:
                    sums_v[rows, :] += total

        def back(i, grad):
            acc[...] += dot_tn(grad[...], weight_v[aligned(i * tile, tile), :])

        tiles = labels // tile
        logits(0, logits_a)
        logits(1, logits_b)
        gradient(0, logits_a, grad_a)

        @pl.loop(1, tiles - 1, step=2)
        def _(i):
            back(i - 1, grad_a)
            logits(i + 1, logits_a)
            gradient(i, logits_b, grad_b)
            back(i, grad_b)
            logits(i + 2, logits_b)
            gradient(i + 1, logits_a, grad_a)

        back(tiles - 2, grad_a)
        gradient(tiles - 1, logits_b, grad_b)
        back(tiles - 1, grad_b)

    fill_mask(ids_near, 0)
    load.wait()
    run_chunk(0, acc_far)
    relays[2].start()
    relays[0].wait()
    relays[1].wait()
    fill_mask(ids_far, 1)
    run_chunk(1, acc_own)

    grad_store = pltpu.make_async_copy(
        grad_v.at[pl.ds(part_rows, labels - part_rows)], grad_hbm, store_sem.at[0]
    )
    grad_store.start()
    embed_out[...] = embed_v[...]

    relays[2].wait()
    for k in range(lane_tiles):
        lanes = slice(k * LANES, (k + 1) * LANES)
        for r in range(docs):
            rows = slice(r * peers, (r + 1) * peers)
            wide32[pl.ds(k * docs + r, peers, stride=ROWS), :] = (
                acc_own[rows, lanes] + acc_relay[rows, lanes]
            )
    for i in range(8):
        step = peers * ROWS // 8
        outgoing[i * step : (i + 1) * step, :] = wide32[i * step : (i + 1) * step, :].astype(BF16)

    @pl.loop(1, peers)
    def _(i):
        peer = lax.rem(chip + i, peers)
        pltpu.make_async_remote_copy(
            src_ref=outgoing.at[aligned(peer * ROWS, ROWS)],
            dst_ref=arrived.at[aligned(chip * ROWS, ROWS)],
            send_sem=scatter_sem.at[0],
            recv_sem=scatter_sem.at[1],
            device_id=device_of(peer, core),
            device_id_type=MESH,
        ).start()

    arrived[aligned(chip * ROWS, ROWS), :] = outgoing[aligned(chip * ROWS, ROWS), :]

    @pl.loop(0, part_rows // part_tile)
    def _(i):
        rows = aligned(i * part_tile, part_tile)
        part_v[rows, :] = jnp.dot(
            grad_v[rows, :], embed_v[...], preferred_element_type=F32
        ).astype(BF16)
        pltpu.make_async_copy(part_v.at[rows], part_hbm.at[rows], store_sem.at[1]).start()

    @pl.loop(0, labels // (8 * LANES))
    def _(i):
        rows = [
            jnp.sum(sums_v[aligned(i * (8 * LANES) + j * LANES, LANES), :].T, axis=0, keepdims=True)
            for j in range(8)
        ]
        bias_grad_ref[aligned(i * 8, 8), :] = jnp.concatenate(rows, axis=0)

    others = (peers - 1) * ROWS
    pltpu.make_async_copy(
        arrived.at[0:others], arrived.at[0:others], scatter_sem.at[1]
    ).wait()
    group = 8

    def add(i, total):
        block = arrived[aligned(i * (group * ROWS), group * ROWS), :].astype(F32)
        for j in range(group):
            total = total + block[j * ROWS : (j + 1) * ROWS, :]
        return total

    total = lax.fori_loop(0, peers // group, add, jnp.zeros((ROWS, LANES), F32))
    for k in range(lane_tiles):
        input_grad_ref[:, k * LANES : (k + 1) * LANES] = total[k * docs : (k + 1) * docs, :]

    pltpu.make_async_copy(
        outgoing.at[0:others], outgoing.at[0:others], scatter_sem.at[0]
    ).wait()
    pltpu.make_async_copy(gathered, gathered, gather_sem.at[0]).wait()
    grad_store.wait()
    pltpu.make_async_copy(part_v, part_hbm, store_sem.at[1]).wait()


def finish_kernel(
    cfg,
    grad_hbm,
    embed_ref,
    part_hbm,
    input_grad_in,
    bias_grad_in,
    input_grad_ref,
    weight_grad_hbm,
    bias_grad_ref,
    grad_v,
    out_v,
    load_sems,
    store_sem,
    part_sem,
):
    part_rows, tile = cfg
    rest = grad_hbm.shape[0]
    tiles = rest // tile

    def load(i):
        rows = aligned(i * tile, tile)
        return pltpu.make_async_copy(grad_hbm.at[rows], grad_v.at[rows], load_sems.at[i])

    for i in range(tiles):
        load(i).start()
    part = pltpu.make_async_copy(part_hbm, weight_grad_hbm.at[pl.ds(0, part_rows)], part_sem)
    part.start()
    input_grad_ref[...] = input_grad_in[...]
    bias_grad_ref[...] = bias_grad_in[...]

    @pl.loop(0, tiles)
    def _(i):
        load(i).wait()
        rows = aligned(i * tile, tile)
        out_v[rows, :] = jnp.dot(
            grad_v[rows, :], embed_ref[...], preferred_element_type=F32
        ).astype(BF16)
        pltpu.make_async_copy(
            out_v.at[rows],
            weight_grad_hbm.at[aligned(part_rows + i * tile, tile)],
            store_sem,
        ).start()

    pltpu.make_async_copy(
        out_v, weight_grad_hbm.at[pl.ds(part_rows, rest)], store_sem
    ).wait()
    part.wait()


def on_device(embeddings, positives, label_weight, label_bias):
    docs, depth = embeddings.shape
    slots = positives.shape[1]
    labels = label_weight.shape[0]
    narrow = lax.axis_size("narrow")
    peers = lax.axis_size("wide") * narrow // 2
    half = docs * peers
    part_rows = labels // 2
    rest = labels - part_rows
    tile, part_tile, rest_tile = 1024, 2048, 1024
    vmem = pl.BlockSpec(memory_space=pltpu.VMEM)
    hbm = pl.BlockSpec(memory_space=pl.ANY)
    shape = jax.ShapeDtypeStruct

    flops = 2 * 2 * labels * 2 * half * depth
    input_grad, bias_grad, grad_rest, embed_all, part = pl.pallas_call(
        functools.partial(
            exchange_kernel, (labels, depth, tile, part_tile, part_rows, peers, narrow)
        ),
        out_shape=[
            shape((docs, depth), F32),
            shape((labels // LANES, LANES), F32),
            shape((rest, 2 * half), BF16),
            shape((2 * half, depth), BF16),
            shape((part_rows, depth), BF16),
        ],
        in_specs=[vmem, vmem, hbm, vmem],
        out_specs=[vmem, vmem, hbm, vmem, hbm],
        scratch_shapes=[
            pltpu.VMEM((labels, depth), BF16),
            pltpu.VMEM((labels, 2 * half), BF16),
            pltpu.VMEM((2 * half, depth), BF16),
            pltpu.VMEM((labels, LANES), F32),
            pltpu.VMEM((labels, LANES), F32),
            pltpu.VMEM((labels // 32, half), jnp.int32),
            pltpu.VMEM((slots, half), jnp.int32),
            pltpu.VMEM((slots, half), jnp.int32),
            pltpu.VMEM((ROWS, LANES), F32),
            pltpu.VMEM((ROWS, LANES), BF16),
            pltpu.VMEM((peers * ROWS, LANES), BF16),
            pltpu.VMEM((peers * ROWS, LANES), F32),
            pltpu.VMEM((tile, half), F32),
            pltpu.VMEM((tile, half), F32),
            pltpu.VMEM((tile, half), BF16),
            pltpu.VMEM((tile, half), BF16),
            pltpu.VMEM((half, depth), F32),
            pltpu.VMEM((half, depth), F32),
            pltpu.VMEM((half, depth), F32),
            pltpu.VMEM((peers * ROWS, LANES), BF16),
            pltpu.VMEM((peers * ROWS, LANES), BF16),
            pltpu.VMEM((part_rows, depth), BF16),
            pltpu.SemaphoreType.DMA,
            pltpu.SemaphoreType.DMA((2,)),
            pltpu.SemaphoreType.DMA((2,)),
            pltpu.SemaphoreType.DMA((6,)),
            pltpu.SemaphoreType.DMA((2,)),
        ],
        compiler_params=pltpu.CompilerParams(
            collective_id=0, has_side_effects=True, vmem_limit_bytes=60 * 2**20
        ),
        cost_estimate=pl.CostEstimate(
            flops=flops, bytes_accessed=labels * depth * 3, transcendentals=0
        ),
        name="exchange",
    )(embeddings, positives, label_weight, label_bias.reshape(labels // LANES, LANES))

    input_grad, weight_grad, bias_grad = pl.pallas_call(
        functools.partial(finish_kernel, (part_rows, rest_tile)),
        out_shape=[
            shape((docs, depth), F32),
            shape((labels, depth), BF16),
            shape((labels // LANES, LANES), F32),
        ],
        in_specs=[hbm, vmem, hbm, vmem, vmem],
        out_specs=[vmem, hbm, vmem],
        scratch_shapes=[
            pltpu.VMEM((rest, 2 * half), BF16),
            pltpu.VMEM((rest, depth), BF16),
            pltpu.SemaphoreType.DMA((rest // rest_tile,)),
            pltpu.SemaphoreType.DMA,
            pltpu.SemaphoreType.DMA,
        ],
        compiler_params=pltpu.CompilerParams(vmem_limit_bytes=48 * 2**20),
        cost_estimate=pl.CostEstimate(
            flops=flops // 4, bytes_accessed=labels * depth * 4, transcendentals=0
        ),
        name="finish",
    )(grad_rest, embed_all, part, input_grad, bias_grad)
    return input_grad, weight_grad, bias_grad.reshape(labels)


def solution(mesh):
    in_specs = (
        P(("wide", "narrow"), None),
        P(("wide", "narrow"), None),
        P(("wide", "narrow"), None),
        P(("wide", "narrow")),
    )
    out_specs = (P(("wide", "narrow"), None), P(("wide", "narrow"), None), P(("wide", "narrow")))
    return jax.shard_map(
        on_device, mesh=mesh, in_specs=in_specs, out_specs=out_specs, check_vma=False
    )
```

```python
import functools

import jax
import jax.numpy as jnp
from jax import lax
from jax.experimental import pallas as pl
from jax.experimental.pallas import tpu as pltpu
from jax.sharding import PartitionSpec as P

LOG2E = 1.4426950408889634
LANES = 128
PART = 3
TILE = 1024
PIECES = 1
MESH = pl.DeviceIdType.MESH
BF16 = jnp.bfloat16
F32 = jnp.float32


def aligned(index, size):
    return pl.ds(pl.multiple_of(index, size), size)


def dot_nt(a, b):
    return lax.dot_general(a, b, (((1,), (1,)), ((), ())), preferred_element_type=F32)


def dot_tn(a, b):
    return lax.dot_general(a, b, (((0,), (0,)), ((), ())), preferred_element_type=F32)


def exchange_kernel(
    cfg,
    embed_ref,
    ids_ref,
    weight_hbm,
    bias_ref,
    input_grad_ref,
    bias_grad_ref,
    grad_v,
    embed_out,
    part_v,
    weight_v,
    embed_v,
    bias_v,
    sums_v,
    mask_v,
    ids_near,
    ids_far,
    message32,
    message,
    ids_message,
    gathered,
    ids_gathered,
    wide32,
    ids_wide32,
    logits_a,
    logits_b,
    grad_a,
    grad_b,
    acc_far,
    acc_own,
    acc_relay,
    outgoing,
    arrived,
    load_sem,
    gather_sem,
    ids_sem,
    relay_sem,
    scatter_sem,
):
    labels, depth, tile, part_tile, part_rows, peers, narrow = cfg
    docs = embed_ref.shape[0]
    slots = ids_ref.shape[1]
    half = docs * peers
    lane_tiles = depth // LANES
    wide_index, narrow_index = lax.axis_index("wide"), lax.axis_index("narrow")
    core = lax.rem(wide_index, 2)
    chip = lax.div(wide_index, 2) * narrow + narrow_index
    label_offset = (wide_index * narrow + narrow_index) * labels
    sibling = (wide_index + 1 - 2 * core, narrow_index)

    def device_of(peer, on_core):
        return (2 * lax.div(peer, narrow) + on_core, lax.rem(peer, narrow))

    barrier = pltpu.get_barrier_semaphore()

    @pl.loop(0, peers)
    def _(i):
        pl.semaphore_signal(
            barrier,
            inc=1,
            device_id=device_of(lax.rem(chip + i, peers), 1 - core),
            device_id_type=MESH,
        )

    load = pltpu.make_async_copy(weight_hbm, weight_v, load_sem)
    load.start()

    embed = embed_ref[...].astype(F32)
    for k in range(lane_tiles):
        message32[k * docs : (k + 1) * docs, :] = embed[:, k * LANES : (k + 1) * LANES]
    ids = ids_ref[...]
    zeros = jnp.zeros((docs, LANES - 2 * slots), F32)
    high = jnp.right_shift(ids, 13).astype(F32)
    middle = (jnp.right_shift(ids, 8) & 31).astype(F32)
    low = (ids & 255).astype(F32)
    message[...] = message32[...].astype(BF16)
    ids_rows = [
        jnp.concatenate([high, middle, zeros], axis=1),
        jnp.concatenate([low, low, zeros], axis=1),
    ]
    ids_message[...] = jnp.concatenate(ids_rows, axis=0).astype(BF16)

    pl.semaphore_wait(barrier, peers)

    for source, target, sems in [
        (message, gathered, gather_sem),
        (ids_message, ids_gathered, ids_sem),
    ]:

        @pl.loop(0, peers)
        def _(i):
            pltpu.make_async_remote_copy(
                src_ref=source,
                dst_ref=target.at[chip],
                send_sem=sems.at[0],
                recv_sem=sems.at[1],
                device_id=device_of(lax.rem(chip + i, peers), 1 - core),
                device_id_type=MESH,
            ).start()

    @pl.loop(0, labels // (8 * LANES))
    def _(i):
        rows = bias_ref[aligned(i * 8, 8), :] * (-LOG2E)
        for j in range(8):
            spread = jnp.broadcast_to(rows[j : j + 1, :], (LANES, LANES)).T
            bias_v[aligned(i * (8 * LANES) + j * LANES, LANES), :] = spread

    pltpu.make_async_copy(gathered, gathered, gather_sem.at[1]).wait()

    rows_of = lane_tiles * docs
    blocks = peers // 8
    for i in range(8):
        wide32[i * blocks * rows_of : (i + 1) * blocks * rows_of, :] = (
            gathered[i * blocks : (i + 1) * blocks].astype(F32).reshape(blocks * rows_of, LANES)
        )

    for k in range(lane_tiles):
        for r in range(docs):
            embed_v[r * peers : (r + 1) * peers, k * LANES : (k + 1) * LANES] = wide32[
                pl.ds(k * docs + r, peers, stride=rows_of), :
            ].astype(BF16)

    relays = [
        pltpu.make_async_remote_copy(
            src_ref=source,
            dst_ref=target,
            send_sem=relay_sem.at[2 * n],
            recv_sem=relay_sem.at[2 * n + 1],
            device_id=sibling,
            device_id_type=MESH,
        )
        for n, (source, target) in enumerate(
            [
                (embed_v.at[0:half], embed_v.at[half : 2 * half]),
                (ids_near, ids_far),
                (acc_far, acc_relay),
            ]
        )
    ]
    relays[0].start()

    def decode_ids():
        pltpu.make_async_copy(ids_gathered, ids_gathered, ids_sem.at[1]).wait()
        ids_wide32[...] = ids_gathered[...].astype(F32).reshape(peers * 2 * docs, LANES)

        def picked(row):
            return ids_wide32[pl.ds(row, peers, stride=2 * docs), :]

        for pair in range(docs // 2):
            first = 2 * pair
            upper = jnp.concatenate([picked(first), picked(first + 1)], axis=0).T
            lower = jnp.concatenate([picked(first + docs), picked(first + docs + 1)], axis=0).T
            whole = upper[:slots] * 8192.0 + upper[slots : 2 * slots] * 256.0 + lower[:slots]
            ids_near[:, pair * LANES : (pair + 1) * LANES] = whole.astype(jnp.int32)
        relays[1].start()

    groups = labels // 32

    def fill_mask(ids_v):
        local = ids_v[...] - label_offset
        local = jnp.where((local >= 0) & (local < labels), local, -1)
        group = jnp.right_shift(local, 5)
        bit = jnp.left_shift(jnp.ones_like(local), local & 31)

        @pl.loop(0, groups // 32)
        def _(i):
            index = lax.broadcasted_iota(jnp.int32, (32, half), 0) + i * 32
            words = jnp.zeros((32, half), jnp.int32)
            for j in range(slots):
                words = words | jnp.where(group[j : j + 1, :] == index, bit[j : j + 1, :], 0)
            mask_v[aligned(i * 32, 32), :] = words

    def run_chunk(chunk, acc, prepare):
        acc[...] = jnp.zeros_like(acc)
        columns = slice(chunk * half, (chunk + 1) * half)

        def logits(i, out):
            out[...] = dot_nt(weight_v[aligned(i * tile, tile), :], embed_v[columns, :])

        def gradient(i, logit, out):
            bits = jnp.left_shift(1, lax.broadcasted_iota(jnp.int32, (32, LANES), 0))
            words = mask_v[aligned(i * (tile // 32), tile // 32), :]
            for g in range(tile // 32):
                rows = aligned(i * tile + g * 32, 32)
                bias = bias_v[rows, :]
                total = None
                for h in range(half // LANES):
                    lanes = slice(h * LANES, (h + 1) * LANES)
                    x = logit[g * 32 : (g + 1) * 32, lanes]
                    sigmoid = pltpu.reciprocal(
                        1.0 + jnp.exp2(x * (-LOG2E) + bias), approx=True
                    )
                    hit = (words[g : g + 1, lanes] & bits) != 0
                    full = sigmoid - jnp.where(hit, 1.0, 0.0)
                    total = full if total is None else total + full
                    rounded = full.astype(BF16)
                    out[g * 32 : (g + 1) * 32, lanes] = rounded
                    grad_v[rows, chunk * half + h * LANES : chunk * half + (h + 1) * LANES] = (
                        rounded
                    )
                if chunk == 0:
                    sums_v[rows, :] = total
                else:
                    sums_v[rows, :] += total

        def back(i, grad):
            acc[...] += dot_tn(grad[...], weight_v[aligned(i * tile, tile), :])

        tiles = labels // tile
        logits(0, logits_a)
        logits(1, logits_b)
        prepare()
        gradient(0, logits_a, grad_a)

        @pl.loop(1, tiles - 1, step=2)
        def _(i):
            back(i - 1, grad_a)
            logits(i + 1, logits_a)
            gradient(i, logits_b, grad_b)
            back(i, grad_b)
            logits(i + 2, logits_b)
            gradient(i + 1, logits_a, grad_a)

        back(tiles - 2, grad_a)
        gradient(tiles - 1, logits_b, grad_b)
        back(tiles - 1, grad_b)

    def prepare_near():
        decode_ids()
        fill_mask(ids_near)

    def prepare_far():
        relays[1].wait()
        fill_mask(ids_far)

    load.wait()
    run_chunk(0, acc_far, prepare_near)
    relays[2].start()
    relays[0].wait()
    run_chunk(1, acc_own, prepare_far)
    embed_out[...] = embed_v[...]

    relays[2].wait()
    for k in range(lane_tiles):
        lanes = slice(k * LANES, (k + 1) * LANES)
        for r in range(docs):
            rows = slice(r * peers, (r + 1) * peers)
            wide32[pl.ds(k * docs + r, peers, stride=rows_of), :] = (
                acc_own[rows, lanes] + acc_relay[rows, lanes]
            )
    for i in range(8):
        outgoing[i * blocks : (i + 1) * blocks] = (
            wide32[i * blocks * rows_of : (i + 1) * blocks * rows_of, :]
            .reshape(blocks, rows_of, LANES)
            .astype(BF16)
        )

    @pl.loop(1, peers)
    def _(step):
        peer = lax.rem(chip + step, peers)
        pltpu.make_async_remote_copy(
            src_ref=outgoing.at[peer],
            dst_ref=arrived.at[chip],
            send_sem=scatter_sem.at[0],
            recv_sem=scatter_sem.at[1],
            device_id=device_of(peer, core),
            device_id_type=MESH,
        ).start()

    arrived[chip] = outgoing[chip]

    @pl.loop(0, part_rows // part_tile)
    def _(i):
        rows = aligned(i * part_tile, part_tile)
        part_v[rows, :] = jnp.dot(
            grad_v[rows, :], embed_v[...], preferred_element_type=F32
        ).astype(BF16)

    @pl.loop(0, labels // (8 * LANES))
    def _(i):
        rows = [
            jnp.sum(sums_v[aligned(i * (8 * LANES) + j * LANES, LANES), :].T, axis=0, keepdims=True)
            for j in range(8)
        ]
        bias_grad_ref[aligned(i * 8, 8), :] = jnp.concatenate(rows, axis=0)

    others = arrived.at[0 : peers - 1]
    pltpu.make_async_copy(others, others, scatter_sem.at[1]).wait()

    def add(i, total):
        return total + jnp.sum(arrived[pl.ds(i * blocks, blocks)].astype(F32), axis=0)

    total = lax.fori_loop(0, 8, add, jnp.zeros((rows_of, LANES), F32))
    for k in range(lane_tiles):
        input_grad_ref[:, k * LANES : (k + 1) * LANES] = total[k * docs : (k + 1) * docs, :]

    others = outgoing.at[0 : peers - 1]
    pltpu.make_async_copy(others, others, scatter_sem.at[0]).wait()
    pltpu.make_async_copy(gathered, gathered, gather_sem.at[0]).wait()
    pltpu.make_async_copy(ids_gathered, ids_gathered, ids_sem.at[0]).wait()


def finish_kernel(
    cfg,
    grad_v,
    embed_v,
    part_v,
    input_grad_in,
    bias_grad_in,
    input_grad_ref,
    weight_grad_hbm,
    bias_grad_ref,
    out_v,
    store_sem,
):
    part_rows, tile = cfg
    labels = weight_grad_hbm.shape[0]
    rest = labels - part_rows
    piece = part_rows // PIECES
    for i in range(PIECES):
        rows = pl.ds(i * piece, piece)
        pltpu.make_async_copy(part_v.at[rows], weight_grad_hbm.at[rows], store_sem.at[0]).start()
    input_grad_ref[...] = input_grad_in[...]
    bias_grad_ref[...] = bias_grad_in[...]

    @pl.loop(0, rest // tile)
    def _(i):
        rows = aligned(i * tile, tile)
        out_v[rows, :] = jnp.dot(
            grad_v[aligned(part_rows + i * tile, tile), :],
            embed_v[...],
            preferred_element_type=F32,
        ).astype(BF16)
        pltpu.make_async_copy(
            out_v.at[rows],
            weight_grad_hbm.at[aligned(part_rows + i * tile, tile)],
            store_sem.at[1],
        ).start()

    pltpu.make_async_copy(
        out_v, weight_grad_hbm.at[pl.ds(part_rows, rest)], store_sem.at[1]
    ).wait()
    pltpu.make_async_copy(
        part_v, weight_grad_hbm.at[pl.ds(0, part_rows)], store_sem.at[0]
    ).wait()


def on_device(embeddings, positives, label_weight, label_bias):
    docs, depth = embeddings.shape
    slots = positives.shape[1]
    labels = label_weight.shape[0]
    narrow = lax.axis_size("narrow")
    peers = lax.axis_size("wide") * narrow // 2
    half = docs * peers
    part_rows = labels * PART // 4
    rest = labels - part_rows
    rows = depth // LANES * docs
    tile, part_tile, rest_tile = TILE, 2048, 1024
    vmem = pl.BlockSpec(memory_space=pltpu.VMEM)
    hbm = pl.BlockSpec(memory_space=pl.ANY)
    shape = jax.ShapeDtypeStruct

    flops = 2 * 2 * labels * 2 * half * depth
    input_grad, bias_grad, grad_all, embed_all, part = pl.pallas_call(
        functools.partial(
            exchange_kernel, (labels, depth, tile, part_tile, part_rows, peers, narrow)
        ),
        out_shape=[
            pltpu.VMEM((docs, depth), F32),
            pltpu.VMEM((labels // LANES, LANES), F32),
            pltpu.VMEM((labels, 2 * half), BF16),
            pltpu.VMEM((2 * half, depth), BF16),
            pltpu.VMEM((part_rows, depth), BF16),
        ],
        in_specs=[vmem, vmem, hbm, vmem],
        out_specs=[vmem] * 5,
        scratch_shapes=[
            pltpu.VMEM((labels, depth), BF16),
            pltpu.VMEM((2 * half, depth), BF16),
            pltpu.VMEM((labels, LANES), F32),
            pltpu.VMEM((labels, LANES), F32),
            pltpu.VMEM((labels // 32, half), jnp.int32),
            pltpu.VMEM((slots, half), jnp.int32),
            pltpu.VMEM((slots, half), jnp.int32),
            pltpu.VMEM((rows, LANES), F32),
            pltpu.VMEM((rows, LANES), BF16),
            pltpu.VMEM((2 * docs, LANES), BF16),
            pltpu.VMEM((peers, rows, LANES), BF16),
            pltpu.VMEM((peers, 2 * docs, LANES), BF16),
            pltpu.VMEM((peers * rows, LANES), F32),
            pltpu.VMEM((peers * 2 * docs, LANES), F32),
            pltpu.VMEM((tile, half), F32),
            pltpu.VMEM((tile, half), F32),
            pltpu.VMEM((tile, half), BF16),
            pltpu.VMEM((tile, half), BF16),
            pltpu.VMEM((half, depth), F32),
            pltpu.VMEM((half, depth), F32),
            pltpu.VMEM((half, depth), F32),
            pltpu.VMEM((peers, rows, LANES), BF16),
            pltpu.VMEM((peers, rows, LANES), BF16),
            pltpu.SemaphoreType.DMA,
            pltpu.SemaphoreType.DMA((2,)),
            pltpu.SemaphoreType.DMA((2,)),
            pltpu.SemaphoreType.DMA((6,)),
            pltpu.SemaphoreType.DMA((2,)),
        ],
        compiler_params=pltpu.CompilerParams(
            collective_id=0, has_side_effects=True, vmem_limit_bytes=44 * 2**20
        ),
        cost_estimate=pl.CostEstimate(
            flops=flops, bytes_accessed=labels * depth * 3, transcendentals=0
        ),
        name="exchange",
    )(embeddings, positives, label_weight, label_bias.reshape(labels // LANES, LANES))

    input_grad, weight_grad, bias_grad = pl.pallas_call(
        functools.partial(finish_kernel, (part_rows, rest_tile)),
        out_shape=[
            shape((docs, depth), F32),
            shape((labels, depth), BF16),
            shape((labels // LANES, LANES), F32),
        ],
        in_specs=[vmem] * 5,
        out_specs=[vmem, hbm, vmem],
        scratch_shapes=[
            pltpu.VMEM((rest, depth), BF16),
            pltpu.SemaphoreType.DMA((2,)),
        ],
        compiler_params=pltpu.CompilerParams(vmem_limit_bytes=8 * 2**20),
        cost_estimate=pl.CostEstimate(
            flops=flops // 4, bytes_accessed=labels * depth * 4, transcendentals=0
        ),
        name="finish",
    )(
        pltpu.with_memory_space_constraint(grad_all, pltpu.VMEM),
        pltpu.with_memory_space_constraint(embed_all, pltpu.VMEM),
        pltpu.with_memory_space_constraint(part, pltpu.VMEM),
        pltpu.with_memory_space_constraint(input_grad, pltpu.VMEM),
        pltpu.with_memory_space_constraint(bias_grad, pltpu.VMEM),
    )
    return input_grad, weight_grad, bias_grad.reshape(labels)


def solution(mesh):
    in_specs = (
        P(("wide", "narrow"), None),
        P(("wide", "narrow"), None),
        P(("wide", "narrow"), None),
        P(("wide", "narrow")),
    )
    out_specs = (P(("wide", "narrow"), None), P(("wide", "narrow"), None), P(("wide", "narrow")))
    return jax.shard_map(
        on_device, mesh=mesh, in_specs=in_specs, out_specs=out_specs, check_vma=False
    )
```

```python
import functools
import itertools

import jax
import jax.numpy as jnp
from jax import lax
from jax.experimental import pallas as pl
from jax.experimental.pallas import tpu as pltpu
from jax.sharding import PartitionSpec as P

LOG2E = 1.4426950408889634
LANES = 128
TILE = 1024
PART = 3
MESH = pl.DeviceIdType.MESH
BF16 = jnp.bfloat16
F32 = jnp.float32


def aligned(index, size):
    return pl.ds(pl.multiple_of(index, size), size)


def dot_nt(a, b):
    return lax.dot_general(a, b, (((1,), (1,)), ((), ())), preferred_element_type=F32)


def dot_tn(a, b):
    return lax.dot_general(a, b, (((0,), (0,)), ((), ())), preferred_element_type=F32)


def exchange_kernel(
    cfg,
    embed_ref,
    ids_ref,
    weight_hbm,
    bias_ref,
    input_grad_ref,
    bias_grad_ref,
    grad_out,
    embed_out,
    part_v,
    weight_v,
    grad_v,
    embed_v,
    bias_v,
    sums_v,
    mask_v,
    ids_near,
    ids_far,
    message32,
    message,
    ids_message,
    gathered,
    ids_gathered,
    wide32,
    ids_wide32,
    logits_a,
    logits_b,
    grad_a,
    grad_b,
    acc_far,
    acc_own,
    acc_relay,
    outgoing,
    arrived,
    load_sem,
    gather_sem,
    ids_sem,
    relay_sem,
    scatter_sem,
    hand_sem,
):
    labels, depth, tile, part_tile, peers, narrow = cfg
    docs = embed_ref.shape[0]
    slots = ids_ref.shape[1]
    half = docs * peers
    lane_tiles = depth // LANES
    wide_index, narrow_index = lax.axis_index("wide"), lax.axis_index("narrow")
    core = lax.rem(wide_index, 2)
    chip = lax.div(wide_index, 2) * narrow + narrow_index
    label_offset = (wide_index * narrow + narrow_index) * labels
    sibling = (wide_index + 1 - 2 * core, narrow_index)

    y, x = lax.rem(lax.div(wide_index, 2), 4), lax.div(narrow_index, 2)
    z_low, z_high = lax.div(wide_index, 8), lax.rem(narrow_index, 2)
    z = z_high * 2 + z_low
    reach = (0, 1, 2, 1)
    steps = itertools.product(range(4), range(4), range(4))
    steps = sorted(steps, key=lambda step: -sum(reach[part] for part in step))
    places = []
    for part in range(4):
        turned = lax.rem(z + part, 4)
        places.append(
            (
                2 * lax.rem(x + part, 4),
                2 * lax.rem(y + part, 4),
                8 * lax.rem(turned, 2),
                lax.div(turned, 2),
            )
        )

    def device_at(step, on_core):
        along_x, along_y, along_z = (places[part] for part in step)
        return (along_z[2] + along_y[1] + on_core, along_x[0] + along_z[3])

    def device_of(peer, on_core):
        return (2 * lax.div(peer, narrow) + on_core, lax.rem(peer, narrow))

    barrier = pltpu.get_barrier_semaphore()

    @pl.loop(0, peers)
    def _(i):
        pl.semaphore_signal(
            barrier,
            inc=1,
            device_id=device_of(lax.rem(chip + i, peers), 1 - core),
            device_id_type=MESH,
        )

    load = pltpu.make_async_copy(weight_hbm, weight_v, load_sem)
    load.start()

    embed = embed_ref[...].astype(F32)
    for k in range(lane_tiles):
        message32[k * docs : (k + 1) * docs, :] = embed[:, k * LANES : (k + 1) * LANES]
    ids = ids_ref[...]
    zeros = jnp.zeros((docs, LANES - 2 * slots), F32)
    high = jnp.right_shift(ids, 13).astype(F32)
    middle = (jnp.right_shift(ids, 8) & 31).astype(F32)
    low = (ids & 255).astype(F32)
    message[...] = message32[...].astype(BF16)
    ids_rows = [
        jnp.concatenate([high, middle, zeros], axis=1),
        jnp.concatenate([low, low, zeros], axis=1),
    ]
    ids_message[...] = jnp.concatenate(ids_rows, axis=0).astype(BF16)

    pl.semaphore_wait(barrier, peers)

    def give(source, target, sems, device):
        pltpu.make_async_remote_copy(
            src_ref=source,
            dst_ref=target.at[chip],
            send_sem=sems.at[0],
            recv_sem=sems.at[1],
            device_id=device,
            device_id_type=MESH,
        ).start()

    for step in steps:
        give(message, gathered, gather_sem, device_at(step, 1 - core))

    @pl.loop(0, peers)
    def _(i):
        peer = lax.rem(chip + i, peers)
        give(ids_message, ids_gathered, ids_sem, device_of(peer, 1 - core))

    @pl.loop(0, labels // (8 * LANES))
    def _(i):
        rows = bias_ref[aligned(i * 8, 8), :] * (-LOG2E)
        for j in range(8):
            spread = jnp.broadcast_to(rows[j : j + 1, :], (LANES, LANES)).T
            bias_v[aligned(i * (8 * LANES) + j * LANES, LANES), :] = spread

    pltpu.make_async_copy(gathered, gathered, gather_sem.at[1]).wait()

    rows_of = lane_tiles * docs
    blocks = peers // 8
    for i in range(8):
        wide32[i * blocks * rows_of : (i + 1) * blocks * rows_of, :] = (
            gathered[i * blocks : (i + 1) * blocks].astype(F32).reshape(blocks * rows_of, LANES)
        )

    for k in range(lane_tiles):
        for r in range(docs):
            embed_v[r * peers : (r + 1) * peers, k * LANES : (k + 1) * LANES] = wide32[
                pl.ds(k * docs + r, peers, stride=rows_of), :
            ].astype(BF16)

    relays = [
        pltpu.make_async_remote_copy(
            src_ref=source,
            dst_ref=target,
            send_sem=relay_sem.at[2 * n],
            recv_sem=relay_sem.at[2 * n + 1],
            device_id=sibling,
            device_id_type=MESH,
        )
        for n, (source, target) in enumerate(
            [
                (embed_v.at[0:half], embed_v.at[half : 2 * half]),
                (ids_near, ids_far),
                (acc_far, acc_relay),
            ]
        )
    ]
    relays[0].start()

    def decode_ids():
        pltpu.make_async_copy(ids_gathered, ids_gathered, ids_sem.at[1]).wait()
        ids_wide32[...] = ids_gathered[...].astype(F32).reshape(peers * 2 * docs, LANES)

        def picked(row):
            return ids_wide32[pl.ds(row, peers, stride=2 * docs), :]

        for pair in range(docs // 2):
            first = 2 * pair
            upper = jnp.concatenate([picked(first), picked(first + 1)], axis=0).T
            lower = jnp.concatenate([picked(first + docs), picked(first + docs + 1)], axis=0).T
            whole = upper[:slots] * 8192.0 + upper[slots : 2 * slots] * 256.0 + lower[:slots]
            ids_near[:, pair * LANES : (pair + 1) * LANES] = whole.astype(jnp.int32)
        relays[1].start()

    def fill_mask(ids_v, chunk):
        local = ids_v[...] - label_offset
        local = jnp.where((local >= 0) & (local < labels), local, -1)
        group = jnp.right_shift(local, 5)
        bit = jnp.left_shift(jnp.ones_like(local), local & 31)

        for i in range(labels // 1024):
            index = lax.broadcasted_iota(jnp.int32, (32, half), 0) + i * 32
            words = jnp.zeros((32, half), jnp.int32)
            for j in range(slots):
                words = words | jnp.where(group[j : j + 1, :] == index, bit[j : j + 1, :], 0)
            mask_v[chunk, i * 32 : (i + 1) * 32, :] = words

    def logits(chunk, i, out):
        out[...] = dot_nt(
            weight_v[aligned(i * tile, tile), :], embed_v[chunk * half : (chunk + 1) * half, :]
        )

    def gradient(chunk, i, logit, out):
        bits = jnp.left_shift(1, lax.broadcasted_iota(jnp.int32, (32, LANES), 0))
        words = mask_v[chunk, aligned(i * (tile // 32), tile // 32), :]
        for g in range(tile // 32):
            rows = aligned(i * tile + g * 32, 32)
            bias = bias_v[rows, :]
            total = None
            for h in range(half // LANES):
                lanes = slice(h * LANES, (h + 1) * LANES)
                x = logit[g * 32 : (g + 1) * 32, lanes]
                sigmoid = pltpu.reciprocal(1.0 + jnp.exp2(x * (-LOG2E) + bias), approx=True)
                hit = (words[g : g + 1, lanes] & bits) != 0
                full = sigmoid - jnp.where(hit, 1.0, 0.0)
                total = full if total is None else total + full
                rounded = full.astype(BF16)
                out[g * 32 : (g + 1) * 32, lanes] = rounded
                start = chunk * half + h * LANES
                grad_v[rows, start : start + LANES] = rounded
            sums_v[chunk, rows, :] = total

    def back(i, grad, acc):
        acc[...] += dot_tn(grad[...], weight_v[aligned(i * tile, tile), :])

    tiles = labels // tile
    acc_far[...] = jnp.zeros_like(acc_far)
    acc_own[...] = jnp.zeros_like(acc_own)
    load.wait()
    logits(0, 0, logits_a)
    logits(0, 1, logits_b)
    decode_ids()
    fill_mask(ids_near, 0)
    gradient(0, 0, logits_a, grad_a)

    def steps_of(chunk, first, last, acc):
        @pl.loop(first, last, step=2)
        def _(i):
            back(i - 1, grad_a, acc)
            logits(chunk, i + 1, logits_a)
            gradient(chunk, i, logits_b, grad_b)
            back(i, grad_b, acc)
            logits(chunk, i + 2, logits_b)
            gradient(chunk, i + 1, logits_a, grad_a)

    steps_of(0, 1, tiles - 1, acc_far)
    relays[0].wait()
    relays[1].wait()
    fill_mask(ids_far, 1)
    back(tiles - 2, grad_a, acc_far)
    logits(1, 0, logits_a)
    gradient(0, tiles - 1, logits_b, grad_b)
    back(tiles - 1, grad_b, acc_far)
    logits(1, 1, logits_b)
    gradient(1, 0, logits_a, grad_a)
    relays[2].start()
    steps_of(1, 1, tiles - 1, acc_own)
    back(tiles - 2, grad_a, acc_own)
    gradient(1, tiles - 1, logits_b, grad_b)
    back(tiles - 1, grad_b, acc_own)

    done = part_v.shape[0]
    hands = [
        pltpu.make_async_copy(grad_v.at[pl.ds(done, labels - done)], grad_out, hand_sem.at[0]),
        pltpu.make_async_copy(embed_v, embed_out, hand_sem.at[1]),
    ]
    for hand in hands:
        hand.start()

    relays[2].wait()
    for k in range(lane_tiles):
        lanes = slice(k * LANES, (k + 1) * LANES)
        for r in range(docs):
            rows = slice(r * peers, (r + 1) * peers)
            wide32[pl.ds(k * docs + r, peers, stride=rows_of), :] = (
                acc_own[rows, lanes] + acc_relay[rows, lanes]
            )
    for i in range(8):
        outgoing[i * blocks : (i + 1) * blocks] = (
            wide32[i * blocks * rows_of : (i + 1) * blocks * rows_of, :]
            .reshape(blocks, rows_of, LANES)
            .astype(BF16)
        )

    for step in steps[:-1]:
        wide_to, narrow_to = device_at(step, core)
        peer = lax.div(wide_to, 2) * narrow + narrow_to
        give(outgoing.at[peer], arrived, scatter_sem, (wide_to, narrow_to))

    arrived[chip] = outgoing[chip]

    @pl.loop(0, done // part_tile)
    def _(i):
        rows = aligned(i * part_tile, part_tile)
        part_v[rows, :] = jnp.dot(
            grad_v[rows, :], embed_v[...], preferred_element_type=F32
        ).astype(BF16)

    def summed(rows):
        return jnp.sum((sums_v[0, rows, :] + sums_v[1, rows, :]).T, axis=0, keepdims=True)

    @pl.loop(0, labels // (8 * LANES))
    def _(i):
        rows = [
            summed(aligned(i * (8 * LANES) + j * LANES, LANES))
            for j in range(8)
        ]
        bias_grad_ref[aligned(i * 8, 8), :] = jnp.concatenate(rows, axis=0)

    others = arrived.at[0 : peers - 1]
    pltpu.make_async_copy(others, others, scatter_sem.at[1]).wait()

    def add(i, total):
        return total + jnp.sum(arrived[pl.ds(i * blocks, blocks)].astype(F32), axis=0)

    total = lax.fori_loop(0, 8, add, jnp.zeros((rows_of, LANES), F32))
    for k in range(lane_tiles):
        input_grad_ref[:, k * LANES : (k + 1) * LANES] = total[k * docs : (k + 1) * docs, :]

    others = outgoing.at[0 : peers - 1]
    pltpu.make_async_copy(others, others, scatter_sem.at[0]).wait()
    for hand in hands:
        hand.wait()
    pltpu.make_async_copy(gathered, gathered, gather_sem.at[0]).wait()
    pltpu.make_async_copy(ids_gathered, ids_gathered, ids_sem.at[0]).wait()


def finish_kernel(
    tile,
    grad_v,
    embed_v,
    part_v,
    input_grad_in,
    bias_grad_in,
    input_grad_ref,
    weight_grad_hbm,
    bias_grad_ref,
    rest_v,
    part_sem,
    rest_sem,
):
    done, rest = part_v.shape[0], rest_v.shape[0]
    part = pltpu.make_async_copy(part_v, weight_grad_hbm.at[pl.ds(0, done)], part_sem)
    part.start()
    input_grad_ref[...] = input_grad_in[...]
    bias_grad_ref[...] = bias_grad_in[...]

    @pl.loop(0, rest // tile)
    def _(i):
        rows = aligned(i * tile, tile)
        rest_v[rows, :] = jnp.dot(
            grad_v[rows, :], embed_v[...], preferred_element_type=F32
        ).astype(BF16)
        pltpu.make_async_copy(
            rest_v.at[rows], weight_grad_hbm.at[aligned(done + i * tile, tile)], rest_sem
        ).start()

    pltpu.make_async_copy(rest_v, weight_grad_hbm.at[pl.ds(done, rest)], rest_sem).wait()
    part.wait()


def on_device(embeddings, positives, label_weight, label_bias):
    docs, depth = embeddings.shape
    slots = positives.shape[1]
    labels = label_weight.shape[0]
    narrow = lax.axis_size("narrow")
    peers = lax.axis_size("wide") * narrow // 2
    half = docs * peers
    rows = depth // LANES * docs
    tile, part_tile = TILE, 2048
    part_rows = labels * PART // 4
    vmem = pl.BlockSpec(memory_space=pltpu.VMEM)
    hbm = pl.BlockSpec(memory_space=pl.ANY)
    shape = jax.ShapeDtypeStruct

    flops = 3 * 2 * labels * 2 * half * depth
    input_grad, bias_grad, grad_rest, embed_all, part = pl.pallas_call(
        functools.partial(
            exchange_kernel, (labels, depth, tile, part_tile, peers, narrow)
        ),
        out_shape=[
            pltpu.VMEM((docs, depth), F32),
            pltpu.VMEM((labels // LANES, LANES), F32),
            pltpu.VMEM((labels - part_rows, 2 * half), BF16),
            pltpu.VMEM((2 * half, depth), BF16),
            pltpu.VMEM((part_rows, depth), BF16),
        ],
        in_specs=[vmem, vmem, hbm, vmem],
        out_specs=[vmem] * 5,
        scratch_shapes=[
            pltpu.VMEM((labels, depth), BF16),
            pltpu.VMEM((labels, 2 * half), BF16),
            pltpu.VMEM((2 * half, depth), BF16),
            pltpu.VMEM((labels, LANES), F32),
            pltpu.VMEM((2, labels, LANES), F32),
            pltpu.VMEM((2, labels // 32, half), jnp.int32),
            pltpu.VMEM((slots, half), jnp.int32),
            pltpu.VMEM((slots, half), jnp.int32),
            pltpu.VMEM((rows, LANES), F32),
            pltpu.VMEM((rows, LANES), BF16),
            pltpu.VMEM((2 * docs, LANES), BF16),
            pltpu.VMEM((peers, rows, LANES), BF16),
            pltpu.VMEM((peers, 2 * docs, LANES), BF16),
            pltpu.VMEM((peers * rows, LANES), F32),
            pltpu.VMEM((peers * 2 * docs, LANES), F32),
            pltpu.VMEM((tile, half), F32),
            pltpu.VMEM((tile, half), F32),
            pltpu.VMEM((tile, half), BF16),
            pltpu.VMEM((tile, half), BF16),
            pltpu.VMEM((half, depth), F32),
            pltpu.VMEM((half, depth), F32),
            pltpu.VMEM((half, depth), F32),
            pltpu.VMEM((peers, rows, LANES), BF16),
            pltpu.VMEM((peers, rows, LANES), BF16),
            pltpu.SemaphoreType.DMA,
            pltpu.SemaphoreType.DMA((2,)),
            pltpu.SemaphoreType.DMA((2,)),
            pltpu.SemaphoreType.DMA((6,)),
            pltpu.SemaphoreType.DMA((2,)),
            pltpu.SemaphoreType.DMA((2,)),
        ],
        compiler_params=pltpu.CompilerParams(
            collective_id=0, has_side_effects=True, vmem_limit_bytes=46 * 2**20
        ),
        cost_estimate=pl.CostEstimate(
            flops=flops, bytes_accessed=labels * depth * 3, transcendentals=0
        ),
        name="exchange",
    )(embeddings, positives, label_weight, label_bias.reshape(labels // LANES, LANES))

    handed = [
        pltpu.with_memory_space_constraint(array, pltpu.VMEM)
        for array in (grad_rest, embed_all, part, input_grad, bias_grad)
    ]
    input_grad, weight_grad, bias_grad = pl.pallas_call(
        functools.partial(finish_kernel, 1024),
        out_shape=[
            shape((docs, depth), F32),
            shape((labels, depth), BF16),
            shape((labels // LANES, LANES), F32),
        ],
        in_specs=[vmem] * 5,
        out_specs=[vmem, hbm, vmem],
        scratch_shapes=[
            pltpu.VMEM((labels - part_rows, depth), BF16),
            pltpu.SemaphoreType.DMA,
            pltpu.SemaphoreType.DMA,
        ],
        compiler_params=pltpu.CompilerParams(vmem_limit_bytes=16 * 2**20),
        cost_estimate=pl.CostEstimate(
            flops=flops // 12, bytes_accessed=labels * depth * 2, transcendentals=0
        ),
        name="finish",
    )(*handed)
    return input_grad, weight_grad, bias_grad.reshape(labels)


def solution(mesh):
    in_specs = (
        P(("wide", "narrow"), None),
        P(("wide", "narrow"), None),
        P(("wide", "narrow"), None),
        P(("wide", "narrow")),
    )
    out_specs = (P(("wide", "narrow"), None), P(("wide", "narrow"), None), P(("wide", "narrow")))
    return jax.shard_map(
        on_device, mesh=mesh, in_specs=in_specs, out_specs=out_specs, check_vma=False
    )
```

```python
import functools
import itertools

import jax
import jax.numpy as jnp
from jax import lax
from jax.experimental import pallas as pl
from jax.experimental.pallas import tpu as pltpu
from jax.sharding import PartitionSpec as P

LOG2E = 1.4426950408889634
LANES = 128
TILE = 1024
UNROLL = 2
PART = 3
MESH = pl.DeviceIdType.MESH
BF16 = jnp.bfloat16
F32 = jnp.float32


def aligned(index, size):
    return pl.ds(pl.multiple_of(index, size), size)


def dot_nt(a, b):
    return lax.dot_general(a, b, (((1,), (1,)), ((), ())), preferred_element_type=F32)


def dot_tn(a, b):
    return lax.dot_general(a, b, (((0,), (0,)), ((), ())), preferred_element_type=F32)


def exchange_kernel(
    cfg,
    embed_ref,
    ids_ref,
    weight_hbm,
    bias_ref,
    input_grad_ref,
    bias_grad_ref,
    grad_out,
    embed_out,
    part_v,
    weight_v,
    grad_v,
    embed_v,
    bias_v,
    sums_v,
    mask_v,
    ids_near,
    ids_far,
    message32,
    message,
    ids_message,
    gathered,
    ids_gathered,
    wide32,
    ids_wide32,
    logits_a,
    logits_b,
    grad_a,
    grad_b,
    acc_far,
    acc_own,
    acc_relay,
    outgoing,
    arrived,
    load_sem,
    gather_sem,
    ids_sem,
    relay_sem,
    scatter_sem,
    hand_sem,
):
    labels, depth, tile, part_tile, peers, narrow = cfg
    docs = embed_ref.shape[0]
    slots = ids_ref.shape[1]
    half = docs * peers
    lane_tiles = depth // LANES
    wide_index, narrow_index = lax.axis_index("wide"), lax.axis_index("narrow")
    core = lax.rem(wide_index, 2)
    chip = lax.div(wide_index, 2) * narrow + narrow_index
    label_offset = (wide_index * narrow + narrow_index) * labels
    sibling = (wide_index + 1 - 2 * core, narrow_index)

    y, x = lax.rem(lax.div(wide_index, 2), 4), lax.div(narrow_index, 2)
    z_low, z_high = lax.div(wide_index, 8), lax.rem(narrow_index, 2)
    z = z_high * 2 + z_low
    reach = (0, 1, 2, 1)
    steps = itertools.product(range(4), range(4), range(4))
    steps = sorted(steps, key=lambda step: -sum(reach[part] for part in step))
    places = []
    for part in range(4):
        turned = lax.rem(z + part, 4)
        places.append(
            (
                2 * lax.rem(x + part, 4),
                2 * lax.rem(y + part, 4),
                8 * lax.rem(turned, 2),
                lax.div(turned, 2),
            )
        )

    def device_at(step, on_core):
        along_x, along_y, along_z = (places[part] for part in step)
        return (along_z[2] + along_y[1] + on_core, along_x[0] + along_z[3])

    def device_of(peer, on_core):
        return (2 * lax.div(peer, narrow) + on_core, lax.rem(peer, narrow))

    barrier = pltpu.get_barrier_semaphore()

    for place in steps:
        pl.semaphore_signal(
            barrier, inc=1, device_id=device_at(place, 1 - core), device_id_type=MESH
        )

    load = pltpu.make_async_copy(weight_hbm, weight_v, load_sem)
    load.start()

    embed = embed_ref[...].astype(F32)
    for k in range(lane_tiles):
        message32[k * docs : (k + 1) * docs, :] = embed[:, k * LANES : (k + 1) * LANES]
    ids = ids_ref[...]
    zeros = jnp.zeros((docs, LANES - 2 * slots), F32)
    high = jnp.right_shift(ids, 13).astype(F32)
    middle = (jnp.right_shift(ids, 8) & 31).astype(F32)
    low = (ids & 255).astype(F32)
    message[...] = message32[...].astype(BF16)
    ids_rows = [
        jnp.concatenate([high, middle, zeros], axis=1),
        jnp.concatenate([low, low, zeros], axis=1),
    ]
    ids_message[...] = jnp.concatenate(ids_rows, axis=0).astype(BF16)

    pl.semaphore_wait(barrier, peers)

    def give(source, target, sems, device):
        pltpu.make_async_remote_copy(
            src_ref=source,
            dst_ref=target.at[chip],
            send_sem=sems.at[0],
            recv_sem=sems.at[1],
            device_id=device,
            device_id_type=MESH,
        ).start()

    for place in steps:
        give(message, gathered, gather_sem, device_at(place, 1 - core))

    @pl.loop(0, peers)
    def _(i):
        peer = lax.rem(chip + i, peers)
        give(ids_message, ids_gathered, ids_sem, device_of(peer, 1 - core))

    @pl.loop(0, labels // (8 * LANES))
    def _(i):
        rows = bias_ref[aligned(i * 8, 8), :] * (-LOG2E)
        for j in range(8):
            spread = jnp.broadcast_to(rows[j : j + 1, :], (LANES, LANES)).T
            bias_v[aligned(i * (8 * LANES) + j * LANES, LANES), :] = spread

    pltpu.make_async_copy(gathered, gathered, gather_sem.at[1]).wait()

    rows_of = lane_tiles * docs
    blocks = peers // 8
    for i in range(8):
        wide32[i * blocks * rows_of : (i + 1) * blocks * rows_of, :] = (
            gathered[i * blocks : (i + 1) * blocks].astype(F32).reshape(blocks * rows_of, LANES)
        )

    for k in range(lane_tiles):
        for r in range(docs):
            embed_v[r * peers : (r + 1) * peers, k * LANES : (k + 1) * LANES] = wide32[
                pl.ds(k * docs + r, peers, stride=rows_of), :
            ].astype(BF16)

    relays = [
        pltpu.make_async_remote_copy(
            src_ref=source,
            dst_ref=target,
            send_sem=relay_sem.at[2 * n],
            recv_sem=relay_sem.at[2 * n + 1],
            device_id=sibling,
            device_id_type=MESH,
        )
        for n, (source, target) in enumerate(
            [
                (embed_v.at[0:half], embed_v.at[half : 2 * half]),
                (ids_near, ids_far),
                (acc_far, acc_relay),
            ]
        )
    ]
    relays[0].start()

    def decode_ids():
        pltpu.make_async_copy(ids_gathered, ids_gathered, ids_sem.at[1]).wait()
        ids_wide32[...] = ids_gathered[...].astype(F32).reshape(peers * 2 * docs, LANES)

        def picked(row):
            return ids_wide32[pl.ds(row, peers, stride=2 * docs), :]

        for pair in range(docs // 2):
            first = 2 * pair
            upper = jnp.concatenate([picked(first), picked(first + 1)], axis=0).T
            lower = jnp.concatenate([picked(first + docs), picked(first + docs + 1)], axis=0).T
            whole = upper[:slots] * 8192.0 + upper[slots : 2 * slots] * 256.0 + lower[:slots]
            ids_near[:, pair * LANES : (pair + 1) * LANES] = whole.astype(jnp.int32)
        relays[1].start()

    def fill_mask(ids_v, chunk):
        local = ids_v[...] - label_offset
        local = jnp.where((local >= 0) & (local < labels), local, -1)
        group = jnp.right_shift(local, 5)
        bit = jnp.left_shift(jnp.ones_like(local), local & 31)

        for i in range(labels // 1024):
            index = lax.broadcasted_iota(jnp.int32, (32, half), 0) + i * 32
            words = jnp.zeros((32, half), jnp.int32)
            for j in range(slots):
                words = words | jnp.where(group[j : j + 1, :] == index, bit[j : j + 1, :], 0)
            mask_v[chunk, i * 32 : (i + 1) * 32, :] = words

    def logits(chunk, i, out):
        out[...] = dot_nt(
            weight_v[aligned(i * tile, tile), :], embed_v[chunk * half : (chunk + 1) * half, :]
        )

    def gradient(chunk, i, logit, out):
        bits = jnp.left_shift(1, lax.broadcasted_iota(jnp.int32, (32, LANES), 0))
        words = mask_v[chunk, aligned(i * (tile // 32), tile // 32), :]
        for g in range(tile // 32):
            rows = aligned(i * tile + g * 32, 32)
            bias = bias_v[rows, :]
            total = None
            for h in range(half // LANES):
                lanes = slice(h * LANES, (h + 1) * LANES)
                x = logit[g * 32 : (g + 1) * 32, lanes]
                sigmoid = pltpu.reciprocal(1.0 + jnp.exp2(x * (-LOG2E) + bias), approx=True)
                hit = (words[g : g + 1, lanes] & bits) != 0
                full = sigmoid - jnp.where(hit, 1.0, 0.0)
                total = full if total is None else total + full
                rounded = full.astype(BF16)
                out[g * 32 : (g + 1) * 32, lanes] = rounded
                start = chunk * half + h * LANES
                grad_v[rows, start : start + LANES] = rounded
            sums_v[chunk, rows, :] = total

    def back(i, grad, acc):
        acc[...] += dot_tn(grad[...], weight_v[aligned(i * tile, tile), :])

    tiles = labels // tile
    acc_far[...] = jnp.zeros_like(acc_far)
    acc_own[...] = jnp.zeros_like(acc_own)
    load.wait()
    logits_of, grads_of, accs = (logits_a, logits_b), (grad_a, grad_b), (acc_far, acc_own)

    def step(now, last=None, following=None, odd=0):
        if last is not None:
            back(last[1], grads_of[1 - odd], accs[last[0]])
        if following is not None:
            logits(*following, logits_of[1 - odd])
        gradient(*now, logits_of[odd], grads_of[odd])

    def steps_of(chunk, first, last):
        @pl.loop(first, last, step=UNROLL)
        def _(i):
            for j in range(UNROLL):
                step((chunk, i + j), (chunk, i + j - 1), (chunk, i + j + 1), (1 + j) % 2)

    logits(0, 0, logits_a)
    logits(0, 1, logits_b)
    decode_ids()
    fill_mask(ids_near, 0)
    step((0, 0))
    steps_of(0, 1, tiles - UNROLL + 1)
    relays[0].wait()
    relays[1].wait()
    fill_mask(ids_far, 1)
    order = [(0, i) for i in range(tiles - UNROLL, tiles)] + [(1, 0), (1, 1)]
    for j in range(1, len(order) - 1):
        step(order[j], order[j - 1], order[j + 1], j % 2)
    relays[2].start()
    steps_of(1, 1, tiles - UNROLL + 1)
    for i in range(tiles - UNROLL + 1, tiles):
        step((1, i), (1, i - 1), (1, i + 1) if i + 1 < tiles else None, i % 2)
    back(tiles - 1, grads_of[(tiles - 1) % 2], acc_own)

    done = part_v.shape[0]
    hands = [
        pltpu.make_async_copy(grad_v.at[pl.ds(done, labels - done)], grad_out, hand_sem.at[0]),
        pltpu.make_async_copy(embed_v, embed_out, hand_sem.at[1]),
    ]
    for hand in hands:
        hand.start()

    relays[2].wait()
    for k in range(lane_tiles):
        lanes = slice(k * LANES, (k + 1) * LANES)
        for r in range(docs):
            rows = slice(r * peers, (r + 1) * peers)
            wide32[pl.ds(k * docs + r, peers, stride=rows_of), :] = (
                acc_own[rows, lanes] + acc_relay[rows, lanes]
            )
    for i in range(8):
        outgoing[i * blocks : (i + 1) * blocks] = (
            wide32[i * blocks * rows_of : (i + 1) * blocks * rows_of, :]
            .reshape(blocks, rows_of, LANES)
            .astype(BF16)
        )

    for place in steps[:-1]:
        wide_to, narrow_to = device_at(place, core)
        peer = lax.div(wide_to, 2) * narrow + narrow_to
        give(outgoing.at[peer], arrived, scatter_sem, (wide_to, narrow_to))

    arrived[chip] = outgoing[chip]

    @pl.loop(0, done // part_tile)
    def _(i):
        rows = aligned(i * part_tile, part_tile)
        part_v[rows, :] = jnp.dot(
            grad_v[rows, :], embed_v[...], preferred_element_type=F32
        ).astype(BF16)

    def summed(rows):
        return jnp.sum((sums_v[0, rows, :] + sums_v[1, rows, :]).T, axis=0, keepdims=True)

    @pl.loop(0, labels // (8 * LANES))
    def _(i):
        rows = [
            summed(aligned(i * (8 * LANES) + j * LANES, LANES))
            for j in range(8)
        ]
        bias_grad_ref[aligned(i * 8, 8), :] = jnp.concatenate(rows, axis=0)

    others = arrived.at[0 : peers - 1]
    pltpu.make_async_copy(others, others, scatter_sem.at[1]).wait()

    def add(i, total):
        return total + jnp.sum(arrived[pl.ds(i * blocks, blocks)].astype(F32), axis=0)

    total = lax.fori_loop(0, 8, add, jnp.zeros((rows_of, LANES), F32))
    for k in range(lane_tiles):
        input_grad_ref[:, k * LANES : (k + 1) * LANES] = total[k * docs : (k + 1) * docs, :]

    others = outgoing.at[0 : peers - 1]
    pltpu.make_async_copy(others, others, scatter_sem.at[0]).wait()
    for hand in hands:
        hand.wait()
    pltpu.make_async_copy(gathered, gathered, gather_sem.at[0]).wait()
    pltpu.make_async_copy(ids_gathered, ids_gathered, ids_sem.at[0]).wait()


def finish_kernel(
    tile,
    grad_v,
    embed_v,
    part_v,
    input_grad_in,
    bias_grad_in,
    input_grad_ref,
    weight_grad_hbm,
    bias_grad_ref,
    rest_v,
    part_sem,
    rest_sem,
):
    done, rest = part_v.shape[0], rest_v.shape[0]
    part = pltpu.make_async_copy(part_v, weight_grad_hbm.at[pl.ds(0, done)], part_sem)
    part.start()
    input_grad_ref[...] = input_grad_in[...]
    bias_grad_ref[...] = bias_grad_in[...]

    @pl.loop(0, rest // tile)
    def _(i):
        rows = aligned(i * tile, tile)
        rest_v[rows, :] = jnp.dot(
            grad_v[rows, :], embed_v[...], preferred_element_type=F32
        ).astype(BF16)
        pltpu.make_async_copy(
            rest_v.at[rows], weight_grad_hbm.at[aligned(done + i * tile, tile)], rest_sem
        ).start()

    pltpu.make_async_copy(rest_v, weight_grad_hbm.at[pl.ds(done, rest)], rest_sem).wait()
    part.wait()


def on_device(embeddings, positives, label_weight, label_bias):
    docs, depth = embeddings.shape
    slots = positives.shape[1]
    labels = label_weight.shape[0]
    narrow = lax.axis_size("narrow")
    peers = lax.axis_size("wide") * narrow // 2
    half = docs * peers
    rows = depth // LANES * docs
    tile, part_tile = TILE, 2048
    part_rows = labels * PART // 4
    vmem = pl.BlockSpec(memory_space=pltpu.VMEM)
    hbm = pl.BlockSpec(memory_space=pl.ANY)
    shape = jax.ShapeDtypeStruct

    flops = 3 * 2 * labels * 2 * half * depth
    input_grad, bias_grad, grad_rest, embed_all, part = pl.pallas_call(
        functools.partial(
            exchange_kernel, (labels, depth, tile, part_tile, peers, narrow)
        ),
        out_shape=[
            pltpu.VMEM((docs, depth), F32),
            pltpu.VMEM((labels // LANES, LANES), F32),
            pltpu.VMEM((labels - part_rows, 2 * half), BF16),
            pltpu.VMEM((2 * half, depth), BF16),
            pltpu.VMEM((part_rows, depth), BF16),
        ],
        in_specs=[vmem, vmem, hbm, vmem],
        out_specs=[vmem] * 5,
        scratch_shapes=[
            pltpu.VMEM((labels, depth), BF16),
            pltpu.VMEM((labels, 2 * half), BF16),
            pltpu.VMEM((2 * half, depth), BF16),
            pltpu.VMEM((labels, LANES), F32),
            pltpu.VMEM((2, labels, LANES), F32),
            pltpu.VMEM((2, labels // 32, half), jnp.int32),
            pltpu.VMEM((slots, half), jnp.int32),
            pltpu.VMEM((slots, half), jnp.int32),
            pltpu.VMEM((rows, LANES), F32),
            pltpu.VMEM((rows, LANES), BF16),
            pltpu.VMEM((2 * docs, LANES), BF16),
            pltpu.VMEM((peers, rows, LANES), BF16),
            pltpu.VMEM((peers, 2 * docs, LANES), BF16),
            pltpu.VMEM((peers * rows, LANES), F32),
            pltpu.VMEM((peers * 2 * docs, LANES), F32),
            pltpu.VMEM((tile, half), F32),
            pltpu.VMEM((tile, half), F32),
            pltpu.VMEM((tile, half), BF16),
            pltpu.VMEM((tile, half), BF16),
            pltpu.VMEM((half, depth), F32),
            pltpu.VMEM((half, depth), F32),
            pltpu.VMEM((half, depth), F32),
            pltpu.VMEM((peers, rows, LANES), BF16),
            pltpu.VMEM((peers, rows, LANES), BF16),
            pltpu.SemaphoreType.DMA,
            pltpu.SemaphoreType.DMA((2,)),
            pltpu.SemaphoreType.DMA((2,)),
            pltpu.SemaphoreType.DMA((6,)),
            pltpu.SemaphoreType.DMA((2,)),
            pltpu.SemaphoreType.DMA((2,)),
        ],
        compiler_params=pltpu.CompilerParams(
            collective_id=0, has_side_effects=True, vmem_limit_bytes=46 * 2**20
        ),
        cost_estimate=pl.CostEstimate(
            flops=flops, bytes_accessed=labels * depth * 3, transcendentals=0
        ),
        name="exchange",
    )(embeddings, positives, label_weight, label_bias.reshape(labels // LANES, LANES))

    handed = [
        pltpu.with_memory_space_constraint(array, pltpu.VMEM)
        for array in (grad_rest, embed_all, part, input_grad, bias_grad)
    ]
    input_grad, weight_grad, bias_grad = pl.pallas_call(
        functools.partial(finish_kernel, 1024),
        out_shape=[
            shape((docs, depth), F32),
            shape((labels, depth), BF16),
            shape((labels // LANES, LANES), F32),
        ],
        in_specs=[vmem] * 5,
        out_specs=[vmem, hbm, vmem],
        scratch_shapes=[
            pltpu.VMEM((labels - part_rows, depth), BF16),
            pltpu.SemaphoreType.DMA,
            pltpu.SemaphoreType.DMA,
        ],
        compiler_params=pltpu.CompilerParams(vmem_limit_bytes=16 * 2**20),
        cost_estimate=pl.CostEstimate(
            flops=flops // 12, bytes_accessed=labels * depth * 2, transcendentals=0
        ),
        name="finish",
    )(*handed)
    return input_grad, weight_grad, bias_grad.reshape(labels)


def solution(mesh):
    in_specs = (
        P(("wide", "narrow"), None),
        P(("wide", "narrow"), None),
        P(("wide", "narrow"), None),
        P(("wide", "narrow")),
    )
    out_specs = (P(("wide", "narrow"), None), P(("wide", "narrow"), None), P(("wide", "narrow")))
    return jax.shard_map(
        on_device, mesh=mesh, in_specs=in_specs, out_specs=out_specs, check_vma=False
    )
```

```python
import functools
import itertools

import jax
import jax.numpy as jnp
from jax import lax
from jax.experimental import pallas as pl
from jax.experimental.pallas import tpu as pltpu
from jax.sharding import PartitionSpec as P

LOG2E = 1.4426950408889634
LANES = 128
TILE = 1024
UNROLL = 2
PART = 3
MESH = pl.DeviceIdType.MESH
BF16 = jnp.bfloat16
F32 = jnp.float32


def aligned(index, size):
    return pl.ds(pl.multiple_of(index, size), size)


def dot_nt(a, b):
    return lax.dot_general(a, b, (((1,), (1,)), ((), ())), preferred_element_type=F32)


def dot_tn(a, b):
    return lax.dot_general(a, b, (((0,), (0,)), ((), ())), preferred_element_type=F32)


def exchange_kernel(
    cfg,
    embed_ref,
    ids_ref,
    weight_hbm,
    bias_ref,
    input_grad_ref,
    bias_grad_ref,
    grad_out,
    embed_out,
    part_v,
    weight_v,
    grad_v,
    embed_v,
    bias_v,
    sums_v,
    mask_v,
    ids_near,
    ids_far,
    message32,
    message,
    ids_message,
    gathered,
    ids_gathered,
    wide32,
    ids_wide32,
    logits_a,
    logits_b,
    grad_a,
    grad_b,
    acc_far,
    acc_own,
    acc_relay,
    outgoing,
    arrived,
    load_sem,
    gather_sem,
    ids_sem,
    relay_sem,
    scatter_sem,
    hand_sem,
):
    labels, depth, tile, part_tile, peers, narrow = cfg
    docs = embed_ref.shape[0]
    slots = ids_ref.shape[1]
    half = docs * peers
    lane_tiles = depth // LANES
    wide_index, narrow_index = lax.axis_index("wide"), lax.axis_index("narrow")
    core = lax.rem(wide_index, 2)
    chip = lax.div(wide_index, 2) * narrow + narrow_index
    label_offset = (wide_index * narrow + narrow_index) * labels
    sibling = (wide_index + 1 - 2 * core, narrow_index)

    y, x = lax.rem(lax.div(wide_index, 2), 4), lax.div(narrow_index, 2)
    z_low, z_high = lax.div(wide_index, 8), lax.rem(narrow_index, 2)
    z = z_high * 2 + z_low
    reach = (0, 1, 2, 1)
    steps = itertools.product(range(4), range(4), range(4))
    steps = sorted(steps, key=lambda step: -sum(reach[part] for part in step))
    places = []
    for part in range(4):
        turned = lax.rem(z + part, 4)
        places.append(
            (
                2 * lax.rem(x + part, 4),
                2 * lax.rem(y + part, 4),
                8 * lax.rem(turned, 2),
                lax.div(turned, 2),
            )
        )

    def device_at(step, on_core):
        along_x, along_y, along_z = (places[part] for part in step)
        return (along_z[2] + along_y[1] + on_core, along_x[0] + along_z[3])

    def device_of(peer, on_core):
        return (2 * lax.div(peer, narrow) + on_core, lax.rem(peer, narrow))

    barrier = pltpu.get_barrier_semaphore()

    for place in steps:
        pl.semaphore_signal(
            barrier, inc=1, device_id=device_at(place, 1 - core), device_id_type=MESH
        )

    load = pltpu.make_async_copy(weight_hbm, weight_v, load_sem)
    load.start()

    embed = embed_ref[...].astype(F32)
    for k in range(lane_tiles):
        message32[k * docs : (k + 1) * docs, :] = embed[:, k * LANES : (k + 1) * LANES]
    ids = ids_ref[...]
    zeros = jnp.zeros((docs, LANES - 2 * slots), F32)
    high = jnp.right_shift(ids, 13).astype(F32)
    middle = (jnp.right_shift(ids, 8) & 31).astype(F32)
    low = (ids & 255).astype(F32)
    message[...] = message32[...].astype(BF16)
    ids_rows = [
        jnp.concatenate([high, middle, zeros], axis=1),
        jnp.concatenate([low, low, zeros], axis=1),
    ]
    ids_message[...] = jnp.concatenate(ids_rows, axis=0).astype(BF16)

    pl.semaphore_wait(barrier, peers)

    def give(source, target, sems, device):
        pltpu.make_async_remote_copy(
            src_ref=source,
            dst_ref=target.at[chip],
            send_sem=sems.at[0],
            recv_sem=sems.at[1],
            device_id=device,
            device_id_type=MESH,
        ).start()

    for place in steps:
        give(message, gathered, gather_sem, device_at(place, 1 - core))

    @pl.loop(0, peers)
    def _(i):
        peer = lax.rem(chip + i, peers)
        give(ids_message, ids_gathered, ids_sem, device_of(peer, 1 - core))

    @pl.loop(0, labels // (8 * LANES))
    def _(i):
        rows = bias_ref[aligned(i * 8, 8), :] * (-LOG2E)
        for j in range(8):
            spread = jnp.broadcast_to(rows[j : j + 1, :], (LANES, LANES)).T
            bias_v[aligned(i * (8 * LANES) + j * LANES, LANES), :] = spread

    pltpu.make_async_copy(gathered, gathered, gather_sem.at[1]).wait()

    rows_of = lane_tiles * docs
    blocks = peers // 8
    for i in range(8):
        wide32[i * blocks * rows_of : (i + 1) * blocks * rows_of, :] = (
            gathered[i * blocks : (i + 1) * blocks].astype(F32).reshape(blocks * rows_of, LANES)
        )

    for k in range(lane_tiles):
        for r in range(docs):
            embed_v[r * peers : (r + 1) * peers, k * LANES : (k + 1) * LANES] = wide32[
                pl.ds(k * docs + r, peers, stride=rows_of), :
            ].astype(BF16)

    relays = [
        pltpu.make_async_remote_copy(
            src_ref=source,
            dst_ref=target,
            send_sem=relay_sem.at[2 * n],
            recv_sem=relay_sem.at[2 * n + 1],
            device_id=sibling,
            device_id_type=MESH,
        )
        for n, (source, target) in enumerate(
            [
                (embed_v.at[0:half], embed_v.at[half : 2 * half]),
                (ids_near, ids_far),
                (acc_far, acc_relay),
            ]
        )
    ]
    relays[0].start()

    def decode_ids():
        pltpu.make_async_copy(ids_gathered, ids_gathered, ids_sem.at[1]).wait()
        ids_wide32[...] = ids_gathered[...].astype(F32).reshape(peers * 2 * docs, LANES)

        def picked(row):
            return ids_wide32[pl.ds(row, peers, stride=2 * docs), :]

        for pair in range(docs // 2):
            first = 2 * pair
            upper = jnp.concatenate([picked(first), picked(first + 1)], axis=0).T
            lower = jnp.concatenate([picked(first + docs), picked(first + docs + 1)], axis=0).T
            whole = upper[:slots] * 8192.0 + upper[slots : 2 * slots] * 256.0 + lower[:slots]
            ids_near[:, pair * LANES : (pair + 1) * LANES] = whole.astype(jnp.int32)
        relays[1].start()

    def fill_mask(ids_v, chunk):
        local = ids_v[...] - label_offset
        local = jnp.where((local >= 0) & (local < labels), local, -1)
        group = jnp.right_shift(local, 5)
        bit = jnp.left_shift(jnp.ones_like(local), local & 31)

        for i in range(labels // 1024):
            index = lax.broadcasted_iota(jnp.int32, (32, half), 0) + i * 32
            words = jnp.zeros((32, half), jnp.int32)
            for j in range(slots):
                words = words | jnp.where(group[j : j + 1, :] == index, bit[j : j + 1, :], 0)
            mask_v[chunk, i * 32 : (i + 1) * 32, :] = words

    def logits(chunk, i, out):
        out[...] = dot_nt(
            weight_v[aligned(i * tile, tile), :], embed_v[chunk * half : (chunk + 1) * half, :]
        )

    def gradient(chunk, i, logit, out):
        bits = jnp.left_shift(1, lax.broadcasted_iota(jnp.int32, (32, LANES), 0))
        words = mask_v[chunk, aligned(i * (tile // 32), tile // 32), :]
        for g in range(tile // 32):
            rows = aligned(i * tile + g * 32, 32)
            bias = bias_v[rows, :]
            total = None
            for h in range(half // LANES):
                lanes = slice(h * LANES, (h + 1) * LANES)
                x = logit[g * 32 : (g + 1) * 32, lanes]
                sigmoid = pltpu.reciprocal(1.0 + jnp.exp2(x * (-LOG2E) + bias), approx=True)
                hit = (words[g : g + 1, lanes] & bits) != 0
                full = sigmoid - jnp.where(hit, 1.0, 0.0)
                total = full if total is None else total + full
                rounded = full.astype(BF16)
                out[g * 32 : (g + 1) * 32, lanes] = rounded
                start = chunk * half + h * LANES
                grad_v[rows, start : start + LANES] = rounded
            sums_v[chunk, rows, :] = total

    def back(i, grad, acc):
        acc[...] += dot_tn(grad[...], weight_v[aligned(i * tile, tile), :])

    tiles = labels // tile
    acc_far[...] = jnp.zeros_like(acc_far)
    acc_own[...] = jnp.zeros_like(acc_own)
    load.wait()
    logits_of, grads_of, accs = (logits_a, logits_b), (grad_a, grad_b), (acc_far, acc_own)

    def step(now, last=None, following=None, odd=0):
        if last is not None:
            back(last[1], grads_of[1 - odd], accs[last[0]])
        if following is not None:
            logits(*following, logits_of[1 - odd])
        gradient(*now, logits_of[odd], grads_of[odd])

    def steps_of(chunk, first, last):
        @pl.loop(first, last, step=UNROLL)
        def _(i):
            for j in range(UNROLL):
                step((chunk, i + j), (chunk, i + j - 1), (chunk, i + j + 1), (1 + j) % 2)

    logits(0, 0, logits_a)
    logits(0, 1, logits_b)
    decode_ids()
    fill_mask(ids_near, 0)
    step((0, 0))
    steps_of(0, 1, tiles - UNROLL + 1)
    relays[0].wait()
    relays[1].wait()
    fill_mask(ids_far, 1)
    order = [(0, i) for i in range(tiles - UNROLL, tiles)] + [(1, 0), (1, 1)]
    for j in range(1, len(order) - 1):
        step(order[j], order[j - 1], order[j + 1], j % 2)
    relays[2].start()
    steps_of(1, 1, tiles - UNROLL + 1)
    for i in range(tiles - UNROLL + 1, tiles):
        step((1, i), (1, i - 1), (1, i + 1) if i + 1 < tiles else None, i % 2)
    back(tiles - 1, grads_of[(tiles - 1) % 2], acc_own)

    done = part_v.shape[0]
    hands = [
        pltpu.make_async_copy(grad_v.at[pl.ds(done, labels - done)], grad_out, hand_sem.at[0]),
        pltpu.make_async_copy(embed_v, embed_out, hand_sem.at[1]),
    ]
    relays[2].wait()
    for k in range(lane_tiles):
        lanes = slice(k * LANES, (k + 1) * LANES)
        for r in range(docs):
            rows = slice(r * peers, (r + 1) * peers)
            wide32[pl.ds(k * docs + r, peers, stride=rows_of), :] = (
                acc_own[rows, lanes] + acc_relay[rows, lanes]
            )
    for i in range(8):
        outgoing[i * blocks : (i + 1) * blocks] = (
            wide32[i * blocks * rows_of : (i + 1) * blocks * rows_of, :]
            .reshape(blocks, rows_of, LANES)
            .astype(BF16)
        )

    for place in steps[:-1]:
        wide_to, narrow_to = device_at(place, core)
        peer = lax.div(wide_to, 2) * narrow + narrow_to
        give(outgoing.at[peer], arrived, scatter_sem, (wide_to, narrow_to))

    arrived[chip] = outgoing[chip]
    for hand in hands:
        hand.start()

    @pl.loop(0, done // part_tile)
    def _(i):
        rows = aligned(i * part_tile, part_tile)
        part_v[rows, :] = jnp.dot(
            grad_v[rows, :], embed_v[...], preferred_element_type=F32
        ).astype(BF16)

    def summed(rows):
        return jnp.sum((sums_v[0, rows, :] + sums_v[1, rows, :]).T, axis=0, keepdims=True)

    @pl.loop(0, labels // (8 * LANES))
    def _(i):
        rows = [
            summed(aligned(i * (8 * LANES) + j * LANES, LANES))
            for j in range(8)
        ]
        bias_grad_ref[aligned(i * 8, 8), :] = jnp.concatenate(rows, axis=0)

    others = arrived.at[0 : peers - 1]
    pltpu.make_async_copy(others, others, scatter_sem.at[1]).wait()

    def add(i, total):
        return total + jnp.sum(arrived[pl.ds(i * blocks, blocks)].astype(F32), axis=0)

    total = lax.fori_loop(0, 8, add, jnp.zeros((rows_of, LANES), F32))
    for k in range(lane_tiles):
        input_grad_ref[:, k * LANES : (k + 1) * LANES] = total[k * docs : (k + 1) * docs, :]

    others = outgoing.at[0 : peers - 1]
    pltpu.make_async_copy(others, others, scatter_sem.at[0]).wait()
    for hand in hands:
        hand.wait()
    pltpu.make_async_copy(gathered, gathered, gather_sem.at[0]).wait()
    pltpu.make_async_copy(ids_gathered, ids_gathered, ids_sem.at[0]).wait()


def finish_kernel(
    tile,
    grad_v,
    embed_v,
    part_v,
    input_grad_in,
    bias_grad_in,
    input_grad_ref,
    weight_grad_hbm,
    bias_grad_ref,
    rest_v,
    part_sem,
    rest_sem,
):
    done, rest = part_v.shape[0], rest_v.shape[0]
    part = pltpu.make_async_copy(part_v, weight_grad_hbm.at[pl.ds(0, done)], part_sem)
    part.start()
    input_grad_ref[...] = input_grad_in[...]
    bias_grad_ref[...] = bias_grad_in[...]

    @pl.loop(0, rest // tile)
    def _(i):
        rows = aligned(i * tile, tile)
        rest_v[rows, :] = jnp.dot(
            grad_v[rows, :], embed_v[...], preferred_element_type=F32
        ).astype(BF16)
        pltpu.make_async_copy(
            rest_v.at[rows], weight_grad_hbm.at[aligned(done + i * tile, tile)], rest_sem
        ).start()

    pltpu.make_async_copy(rest_v, weight_grad_hbm.at[pl.ds(done, rest)], rest_sem).wait()
    part.wait()


def on_device(embeddings, positives, label_weight, label_bias):
    docs, depth = embeddings.shape
    slots = positives.shape[1]
    labels = label_weight.shape[0]
    narrow = lax.axis_size("narrow")
    peers = lax.axis_size("wide") * narrow // 2
    half = docs * peers
    rows = depth // LANES * docs
    tile, part_tile = TILE, 3072
    part_rows = labels * PART // 4
    vmem = pl.BlockSpec(memory_space=pltpu.VMEM)
    hbm = pl.BlockSpec(memory_space=pl.ANY)
    shape = jax.ShapeDtypeStruct

    flops = 3 * 2 * labels * 2 * half * depth
    input_grad, bias_grad, grad_rest, embed_all, part = pl.pallas_call(
        functools.partial(
            exchange_kernel, (labels, depth, tile, part_tile, peers, narrow)
        ),
        out_shape=[
            pltpu.VMEM((docs, depth), F32),
            pltpu.VMEM((labels // LANES, LANES), F32),
            pltpu.VMEM((labels - part_rows, 2 * half), BF16),
            pltpu.VMEM((2 * half, depth), BF16),
            pltpu.VMEM((part_rows, depth), BF16),
        ],
        in_specs=[vmem, vmem, hbm, vmem],
        out_specs=[vmem] * 5,
        scratch_shapes=[
            pltpu.VMEM((labels, depth), BF16),
            pltpu.VMEM((labels, 2 * half), BF16),
            pltpu.VMEM((2 * half, depth), BF16),
            pltpu.VMEM((labels, LANES), F32),
            pltpu.VMEM((2, labels, LANES), F32),
            pltpu.VMEM((2, labels // 32, half), jnp.int32),
            pltpu.VMEM((slots, half), jnp.int32),
            pltpu.VMEM((slots, half), jnp.int32),
            pltpu.VMEM((rows, LANES), F32),
            pltpu.VMEM((rows, LANES), BF16),
            pltpu.VMEM((2 * docs, LANES), BF16),
            pltpu.VMEM((peers, rows, LANES), BF16),
            pltpu.VMEM((peers, 2 * docs, LANES), BF16),
            pltpu.VMEM((peers * rows, LANES), F32),
            pltpu.VMEM((peers * 2 * docs, LANES), F32),
            pltpu.VMEM((tile, half), F32),
            pltpu.VMEM((tile, half), F32),
            pltpu.VMEM((tile, half), BF16),
            pltpu.VMEM((tile, half), BF16),
            pltpu.VMEM((half, depth), F32),
            pltpu.VMEM((half, depth), F32),
            pltpu.VMEM((half, depth), F32),
            pltpu.VMEM((peers, rows, LANES), BF16),
            pltpu.VMEM((peers, rows, LANES), BF16),
            pltpu.SemaphoreType.DMA,
            pltpu.SemaphoreType.DMA((2,)),
            pltpu.SemaphoreType.DMA((2,)),
            pltpu.SemaphoreType.DMA((6,)),
            pltpu.SemaphoreType.DMA((2,)),
            pltpu.SemaphoreType.DMA((2,)),
        ],
        compiler_params=pltpu.CompilerParams(
            collective_id=0, has_side_effects=True, vmem_limit_bytes=46 * 2**20
        ),
        cost_estimate=pl.CostEstimate(
            flops=flops, bytes_accessed=labels * depth * 3, transcendentals=0
        ),
        name="exchange",
    )(embeddings, positives, label_weight, label_bias.reshape(labels // LANES, LANES))

    handed = [
        pltpu.with_memory_space_constraint(array, pltpu.VMEM)
        for array in (grad_rest, embed_all, part, input_grad, bias_grad)
    ]
    input_grad, weight_grad, bias_grad = pl.pallas_call(
        functools.partial(finish_kernel, 1024),
        out_shape=[
            shape((docs, depth), F32),
            shape((labels, depth), BF16),
            shape((labels // LANES, LANES), F32),
        ],
        in_specs=[vmem] * 5,
        out_specs=[vmem, hbm, vmem],
        scratch_shapes=[
            pltpu.VMEM((labels - part_rows, depth), BF16),
            pltpu.SemaphoreType.DMA,
            pltpu.SemaphoreType.DMA,
        ],
        compiler_params=pltpu.CompilerParams(vmem_limit_bytes=16 * 2**20),
        cost_estimate=pl.CostEstimate(
            flops=flops // 12, bytes_accessed=labels * depth * 2, transcendentals=0
        ),
        name="finish",
    )(*handed)
    return input_grad, weight_grad, bias_grad.reshape(labels)


def solution(mesh):
    in_specs = (
        P(("wide", "narrow"), None),
        P(("wide", "narrow"), None),
        P(("wide", "narrow"), None),
        P(("wide", "narrow")),
    )
    out_specs = (P(("wide", "narrow"), None), P(("wide", "narrow"), None), P(("wide", "narrow")))
    return jax.shard_map(
        on_device, mesh=mesh, in_specs=in_specs, out_specs=out_specs, check_vma=False
    )
```
